128 devices in a mesh: left: 8 (over y, x_hi), right: 16 (over x_lo, z, core).
Axes of the slice: x: 4 (x_hi: 2, x_lo: 2; x = x_hi * 2 + x_lo), y: 4, z: 4, core: 2. Of those that a mesh axis runs over, the one named last changes fastest.
Arguments:
- state: float32 [128, 1024, 1024], P(('left', 'right')), may hold values from -20 to 20
- left_env: bfloat16 [2, 128, 1024, 1024], P(None, ('left', 'right')), may hold values from -0.5 to 2.5
- right_env: bfloat16 [2, 128, 1024, 1024], P(None, ('left', 'right')), may hold values from -0.5 to 2.5
- site_ops: float32 [2, 4, 4], replicated, may hold values from -3 to 3
- left_live: int32 [32], replicated, may hold values from 1 to 4
- right_live: int32 [34], replicated, may hold values from 1 to 4
Outputs:
- next_vector: float32 [128, 1024, 1024], P(('left', 'right'))
- coefficients: float32 [2], replicated
The draws below stay inside these ranges and needn't reach their ends.
All inputs are finite; a program needn't handle non-finite values.
Results may differ from the reference program's by a relative error of at most 0.0047.
Values may be sent and summed in bfloat16 or wider, within the bound.
A program may use at most 64 MiB of HBM per device.

```python
import jax
import jax.numpy as jnp
from jax import lax

BLOCK = 256
SEC_BLOCKS = 4
PAIR = 4
SEC = 1024
SECTORS = 32
RSECTORS = 34
BLOCKS = 128


def env_blocks(key, count):
    rows = jnp.arange(SEC, dtype=jnp.int32)
    identity = (rows[:, None] == rows[None, :]).astype(jnp.float32)
    spread = jnp.clip(jax.random.normal(key, (2, count, SEC, SEC), jnp.float32), -6.0, 6.0)
    diagonal = jax.random.uniform(jax.random.fold_in(key, 1), (2, count, 1, SEC), jnp.float32, 0.5, 1.5)
    return spread * (0.6 / SEC ** 0.5) + identity * diagonal


def draw_left_env(key, part):
    base = env_blocks(jax.random.fold_in(key, 5), SECTORS)
    return jnp.repeat(base, PAIR, axis=1).astype(jnp.bfloat16)


def draw_right_env(key, part):
    base = env_blocks(jax.random.fold_in(key, 7), SECTORS + 2)
    block_ids = jnp.arange(BLOCKS, dtype=jnp.int32)
    index = (block_ids // PAIR + (block_ids % PAIR + 1) // 2).astype(jnp.int32)
    return jnp.take(base, index, axis=1).astype(jnp.bfloat16)


def draw_state(key, part):
    place = jnp.arange(BLOCKS, dtype=jnp.float32) / BLOCKS
    ramp = jnp.exp(0.6 * place)[:, None, None]
    values = jnp.clip(jax.random.normal(key, (BLOCKS, SEC, SEC), jnp.float32), -6.0, 6.0)
    return (values * ramp).astype(jnp.float32)


def touch_ends(result, own_key, low, high):
    longest = result.shape.index(max(result.shape))
    spots = []
    for shift in (0, 1):
        where = [jax.random.randint(jax.random.fold_in(own_key, axis), (), 0, length) for axis, length in enumerate(result.shape)]
        where[longest] = (where[longest] + shift) % result.shape[longest]
        spots.append(tuple(where))
    return result.at[spots[0]].set(low).at[spots[1]].set(high)


def scatter_about(stream_key, extent, scale, bound, held_as=jnp.bfloat16):
    values = jax.random.normal(stream_key, extent, jnp.float32) * scale
    return jnp.minimum(jnp.maximum(values, -bound), bound).astype(held_as)


def setup_inputs(seed: int = 0) -> dict:
    streams_of = jax.random.split(jax.random.key(seed), 7)
    state = draw_state(jax.random.fold_in(streams_of[6], 71), 0)
    left_env = draw_left_env(jax.random.fold_in(streams_of[6], 71), 0)
    right_env = draw_right_env(jax.random.fold_in(streams_of[6], 71), 0)
    site_ops = scatter_about(streams_of[3], (2, PAIR, PAIR), PAIR ** -0.5, 3.0, jnp.float32)
    left_live = touch_ends(jax.random.randint(streams_of[4], (SECTORS,), 1, SEC_BLOCKS + 1), jax.random.fold_in(streams_of[4], 1), 1, SEC_BLOCKS).astype(jnp.int32)
    right_live = touch_ends(jax.random.randint(streams_of[5], (RSECTORS,), 1, SEC_BLOCKS + 1), jax.random.fold_in(streams_of[5], 1), 1, SEC_BLOCKS).astype(jnp.int32)
    return {"state": state, "left_env": left_env, "right_env": right_env, "site_ops": site_ops, "left_live": left_live, "right_live": right_live}


def pair_steps():
    return ((jnp.arange(PAIR, dtype=jnp.int32) + 1) // 2).astype(jnp.int32)

def source_weight(site_ops, target, offset):
    own_pair = (target % PAIR).astype(jnp.int32)
    source_pair = ((own_pair - offset) % PAIR).astype(jnp.int32)
    valid = target >= offset
    return jnp.where(valid, site_ops[0, own_pair, source_pair], jnp.zeros((), site_ops.dtype))

def reference(state, left_env, right_env, site_ops, left_live, right_live):
    steps = pair_steps()
    block_ids = jnp.arange(BLOCKS, dtype=jnp.int32)
    sectors = (block_ids // PAIR).astype(jnp.int32)
    pair_of = (block_ids % PAIR).astype(jnp.int32)
    row_live = left_live[sectors] * BLOCK
    col_live = right_live[sectors + steps[pair_of]] * BLOCK
    positions = jnp.arange(SEC, dtype=jnp.int32)
    row_mask = (positions[None, :] < row_live[:, None]).astype(jnp.float32)
    col_mask = (positions[None, :] < col_live[:, None]).astype(jnp.float32)
    entries = float(BLOCKS * SEC * SEC)
    masked = state * row_mask[:, :, None] * col_mask[:, None, :]
    vector = masked / jnp.sqrt(jnp.sum(masked * masked) / entries + 1e-06)
    rounded = vector.astype(jnp.bfloat16)

    def one_block(target):
        own = lax.dynamic_index_in_dim(rounded, target, 0, keepdims=False)
        two = lax.dynamic_index_in_dim(rounded, jnp.maximum(target - 2, 0).astype(jnp.int32), 0, keepdims=False)
        three = lax.dynamic_index_in_dim(rounded, jnp.maximum(target - 3, 0).astype(jnp.int32), 0, keepdims=False)
        weight_two = source_weight(site_ops, target, 2)
        weight_three = source_weight(site_ops, target, 3)
        source = (weight_two * two.astype(jnp.float32) + weight_three * three.astype(jnp.float32)).astype(jnp.bfloat16)
        right_zero = lax.dynamic_index_in_dim(right_env[0], target, 0, keepdims=False)
        right_one = lax.dynamic_index_in_dim(right_env[1], target, 0, keepdims=False)
        left_zero = lax.dynamic_index_in_dim(left_env[0], target, 0, keepdims=False)
        left_one = lax.dynamic_index_in_dim(left_env[1], target, 0, keepdims=False)
        part_zero = jnp.dot(source, right_zero, preferred_element_type=jnp.float32).astype(jnp.bfloat16)
        part_one = jnp.dot(own, right_one, preferred_element_type=jnp.float32).astype(jnp.bfloat16)
        own_pair = (target % PAIR).astype(jnp.int32)
        diag_weight = site_ops[1, own_pair, own_pair]
        image = jnp.dot(left_zero, part_zero, preferred_element_type=jnp.float32)
        image = image + diag_weight * jnp.dot(left_one, part_one, preferred_element_type=jnp.float32)
        rows = lax.dynamic_index_in_dim(row_mask, target, 0, keepdims=False)
        cols = lax.dynamic_index_in_dim(col_mask, target, 0, keepdims=False)
        return image * rows[:, None] * cols[None, :]
    image = lax.map(one_block, block_ids)
    alpha_value = jnp.sum(vector * image) / entries
    residual = image - alpha_value * vector
    beta_value = jnp.sqrt(jnp.sum(residual * residual) / entries + 1e-06)
    return (residual / beta_value, jnp.stack([alpha_value, beta_value]).astype(jnp.float32))
```

```python
import jax
import jax.numpy as jnp
from jax import lax
from jax.experimental import pallas as pl
from jax.experimental.pallas import tpu as pltpu
from jax.sharding import PartitionSpec as P

MESH = pl.DeviceIdType.MESH
BLOCK = 256
PAIR = 4
SEC = 1024
DEVICES = 128
CHUNK = 32
CHUNKS = SEC // CHUNK
MERGED_UP = 13
LOAD = 128
LOADS = SEC // LOAD
TILE = 256
TILES = SEC // TILE
PHASES = ((1, 16), (16, 8))


def own_block():
    return lax.axis_index("left") * 16 + lax.axis_index("right")


def place(block):
    block = lax.rem(block + DEVICES, DEVICES)
    return (lax.div(block, 16), lax.rem(block, 16))


def along_z(block, step, core):
    z = lax.rem(lax.div(block, 2), 4)
    return lax.div(block, 8) * 8 + lax.rem(z + step + 4, 4) * 2 + core


def group_peer(block, stride, size, step):
    digit = lax.rem(lax.div(block, stride), size)
    return block + (lax.rem(digit + step, size) - digit) * stride


def goes_up(chunk):
    return lax.div((chunk + 1) * MERGED_UP, CHUNKS) > lax.div(chunk * MERGED_UP, CHUNKS)


def step_kernel(
    site_ops, left_live, right_live, state, left_env, right_env,
    image, masked, sums,
    own, first, second, source, left_zero, left_one, right_zero, right_one, part,
    slots, share, load_sem, env_sem, first_sem, second_sem, source_sem, send_sem, sum_send, sum_recv,
):
    k = own_block()
    core = lax.rem(k, 2)
    is_low = core == 0
    is_high = core == 1

    loads = [
        pltpu.make_async_copy(
            state.at[0, pl.ds(i * LOAD, LOAD)], masked.at[pl.ds(i * LOAD, LOAD)], load_sem.at[i]
        )
        for i in range(LOADS)
    ]
    for load in loads:
        load.start()
    envs = [
        pltpu.make_async_copy(right_env.at[1, 0], right_one, env_sem.at[0]),
        pltpu.make_async_copy(left_env.at[1, 0], left_one, env_sem.at[1]),
        pltpu.make_async_copy(right_env.at[0, 0], right_zero, env_sem.at[2]),
        pltpu.make_async_copy(left_env.at[0, 0], left_zero, env_sem.at[3]),
    ]
    for env in envs:
        env.start()

    barrier = pltpu.get_barrier_semaphore()

    def greet(block):
        pl.semaphore_signal(barrier, inc=1, device_id=place(block), device_id_type=MESH)

    relay = along_z(k, -1, 0)
    onward = along_z(k, 1, 1) + 3
    @pl.when(is_low)
    def _():
        greet(k - 1)
        greet(k - 2)
        greet(along_z(k, 1, 1))
        greet(along_z(k - 3 + DEVICES, -1, 0))

    @pl.when(is_high)
    def _():
        greet(k - 1)
        greet(k + 1)
        greet(k - 2)

    partners = 0
    for stride, size in PHASES:
        for step in range(1, size):
            greet(group_peer(k, stride, size, step))
            partners += 1

    def weight(target, distance):
        target = lax.rem(target + DEVICES, DEVICES)
        pair = lax.rem(target, PAIR)
        entry = site_ops[0, pair, lax.rem(pair - distance + PAIR, PAIR)]
        return jnp.where(target >= distance, entry, 0.0)

    up_two = weight(k + 2, 2)
    up_three = weight(k + 2, 3)
    merge_own = jnp.where(is_low, up_two, weight(k + 3, 3))
    merge_other = jnp.where(is_low, up_three, weight(k + 3, 2))
    own_pair = lax.rem(k, PAIR)
    diagonal = site_ops[1, own_pair, own_pair]
    sector = lax.div(k, PAIR)
    rows = left_live[sector] * BLOCK
    columns = right_live[sector + lax.div(own_pair + 1, 2)] * BLOCK
    column_live = lax.broadcasted_iota(jnp.int32, (1, SEC), 1) < columns

    def live(first_row, count):
        return (
            lax.broadcasted_iota(jnp.int32, (count, 1), 0) + first_row < rows
        ) & column_live

    def chunk_of(ref, chunk):
        return ref.at[pl.ds(pl.multiple_of(chunk * CHUNK, CHUNK), CHUNK)]

    def send(src, dst, send_at, recv, chunk, target):
        pltpu.make_async_remote_copy(
            src_ref=chunk_of(src, chunk),
            dst_ref=chunk_of(dst, chunk),
            send_sem=send_sem.at[send_at],
            recv_sem=recv.at[chunk],
            device_id=place(target),
            device_id_type=MESH,
        ).start()

    def arrived(ref, recv, chunk):
        pltpu.make_async_copy(chunk_of(ref, chunk), chunk_of(ref, chunk), recv.at[chunk]).wait()

    def fold(values):
        return jnp.sum(values.reshape(-1, 8, SEC // 128, 128), axis=(0, 2))

    share[...] = jnp.zeros_like(share)
    for i in range(LOADS):
        loads[i].wait()
        at = pl.ds(i * LOAD, LOAD)
        values = jnp.where(live(i * LOAD, LOAD), masked[at], 0.0)
        masked[at] = values
        own[at] = values.astype(jnp.bfloat16)
        share[0] += jnp.sum((values * values).reshape(LOAD // 8, 8, SEC), axis=0)
        if i == 0:
            pl.semaphore_wait(barrier, 4 - core + partners)

        @pl.loop(i * (LOAD // CHUNK), (i + 1) * (LOAD // CHUNK))
        def _(chunk):
            @pl.when(is_low)
            def _():
                send(own, first, 0, first_sem, chunk, k + 1)

                @pl.when(jnp.logical_not(goes_up(chunk)))
                def _():
                    send(own, second, 1, second_sem, chunk, k - 1)

            @pl.when(is_high & goes_up(chunk))
            def _():
                send(own, second, 1, second_sem, chunk, k + 1)

    @pl.when(is_high)
    def _():
        @pl.loop(0, CHUNKS)
        def _(chunk):
            arrived(first, first_sem, chunk)
            at = pl.ds(pl.multiple_of(chunk * CHUNK, CHUNK), CHUNK)
            first[at] = (
                up_two * own[at].astype(jnp.float32) + up_three * first[at].astype(jnp.float32)
            ).astype(jnp.bfloat16)
            send(first, source, 2, source_sem, chunk, k + 2)

    def tile_at(index):
        return pl.ds(pl.multiple_of(index * TILE, TILE), TILE)

    def part_one(index):
        at = tile_at(index)
        part[at] = jnp.dot(
            own[at], right_one[...], preferred_element_type=jnp.float32
        ).astype(jnp.bfloat16)

    def image_one(index):
        at = tile_at(index)
        image[at] = diagonal * jnp.dot(left_one[at], part[...], preferred_element_type=jnp.float32)

    def exchange(chunk):
        up = goes_up(chunk)

        @pl.when(up == is_low)
        def _():
            arrived(second, second_sem, chunk)
            at = pl.ds(pl.multiple_of(chunk * CHUNK, CHUNK), CHUNK)
            second[at] = (
                merge_own * own[at].astype(jnp.float32)
                + merge_other * second[at].astype(jnp.float32)
            ).astype(jnp.bfloat16)

            @pl.when(is_low)
            def _():
                send(second, source, 2, source_sem, chunk, k + 2)

            @pl.when(is_high)
            def _():
                send(second, first, 3, first_sem, chunk, relay)

        @pl.when(is_low & jnp.logical_not(up))
        def _():
            arrived(first, first_sem, chunk)
            send(first, source, 3, source_sem, chunk, onward)

    @pl.loop(0, TILES)
    def _(index):
        @pl.when(index == 0)
        def _():
            envs[0].wait()
            envs[1].wait()
            envs[2].wait()
            envs[3].wait()

        part_one(index)
        exchange(2 * index)
        exchange(2 * index + 1)

    @pl.loop(0, TILES)
    def _(index):
        image_one(index)
        exchange(2 * index + 8)
        exchange(2 * index + 9)

    per_tile = TILE // CHUNK

    def consume(index, last):
        @pl.loop(index * per_tile, (index + 1) * per_tile)
        def _(chunk):
            arrived(source, source_sem, chunk)

        piece = pl.ds(index * TILE, TILE)
        part[piece] = jnp.dot(
            source[piece], right_zero[...], preferred_element_type=jnp.float32
        ).astype(jnp.bfloat16)

        @pl.loop(0, TILES)
        def _(row):
            at = tile_at(row)
            values = image[at] + jnp.dot(
                left_zero[at, piece], part[piece], preferred_element_type=jnp.float32
            )
            if last:
                values = jnp.where(live(row * TILE, TILE), values, 0.0)
                share[1] += jnp.sum((values * masked[at]).reshape(TILE // 8, 8, SEC), axis=0)
                share[2] += jnp.sum((values * values).reshape(TILE // 8, 8, SEC), axis=0)
            image[at] = values

    consume(0, False)

    @pl.loop(16, 24)
    def _(chunk):
        exchange(chunk)

    consume(1, False)

    @pl.loop(24, 32)
    def _(chunk):
        exchange(chunk)

    consume(2, False)
    consume(3, True)

    for phase, (stride, size) in enumerate(PHASES):
        digit = lax.rem(lax.div(k, stride), size)
        if phase == 0:
            total = jnp.sum(share[...].reshape(3, 8, SEC // 128, 128), axis=2)
        else:
            total = jnp.sum(slots[phase - 1, 0 : PHASES[phase - 1][1]], axis=0)
        slots[phase, digit] = total
        for step in range(1, size):
            pltpu.make_async_remote_copy(
                src_ref=slots.at[phase, digit],
                dst_ref=slots.at[phase, digit],
                send_sem=sum_send.at[phase],
                recv_sem=sum_recv.at[phase],
                device_id=place(group_peer(k, stride, size, step)),
                device_id_type=MESH,
            ).start()
        others = slots.at[phase, pl.ds(0, size - 1)]
        pltpu.make_async_copy(others, others, sum_recv.at[phase]).wait()
        pltpu.make_async_copy(others, others, sum_send.at[phase]).wait()
    total = jnp.sum(slots[len(PHASES) - 1, 0 : PHASES[-1][1]], axis=0)
    total = jnp.sum(jnp.sum(total, axis=2, keepdims=True), axis=1, keepdims=True)
    entries = float(DEVICES * SEC * SEC)
    start = total[0] / entries
    overlap = total[1] / entries
    square = total[2] / entries
    scale = 1.0 / jnp.sqrt(start + 1e-06)
    slope = scale * scale * overlap
    rest = square - 2.0 * slope * overlap + slope * slope * start
    beta = jnp.sqrt(scale * scale * jnp.maximum(rest, 0.0) + 1e-06)
    sums[0] = jnp.broadcast_to(slope, (8, 128))
    sums[1] = jnp.broadcast_to(scale / beta, (8, 128))
    sums[2] = jnp.broadcast_to(beta, (8, 128))

    def sent(flow, chunks):
        piece = own.at[pl.ds(0, chunks * CHUNK)]
        pltpu.make_async_copy(piece, piece, send_sem.at[flow]).wait()

    @pl.when(is_low)
    def _():
        sent(0, CHUNKS)
        sent(1, CHUNKS - MERGED_UP)
        sent(2, MERGED_UP)
        sent(3, CHUNKS - MERGED_UP)

    @pl.when(is_high)
    def _():
        sent(1, MERGED_UP)
        sent(2, CHUNKS)
        sent(3, CHUNKS - MERGED_UP)


def finish_kernel(sums, image, masked, next_vector, coefficients):
    slope = sums[0, 0:1, 0:1]
    gain = sums[1, 0:1, 0:1]
    next_vector[0] = (image[...] - slope * masked[...]) * gain
    coefficients[0] = jnp.max(sums[0])
    coefficients[1] = jnp.max(sums[2])


def per_device(state, left_env, right_env, site_ops, left_live, right_live):
    hbm = pl.BlockSpec(memory_space=pltpu.HBM)
    smem = pl.BlockSpec(memory_space=pltpu.SMEM)
    vmem = pl.BlockSpec(memory_space=pltpu.VMEM)
    block = pltpu.VMEM((SEC, SEC), jnp.bfloat16)
    dma = pltpu.SemaphoreType.DMA
    image, masked, sums = pl.pallas_call(
        step_kernel,
        out_shape=(
            jax.ShapeDtypeStruct((SEC, SEC), jnp.float32),
            jax.ShapeDtypeStruct((SEC, SEC), jnp.float32),
            jax.ShapeDtypeStruct((3, 8, 128), jnp.float32),
        ),
        in_specs=[smem, smem, smem, hbm, hbm, hbm],
        out_specs=(vmem, vmem, vmem),
        scratch_shapes=[
            block, block, block, block, block, block, block, block, block,
            pltpu.VMEM((len(PHASES), max(size for _, size in PHASES), 3, 8, 128), jnp.float32),
            pltpu.VMEM((3, 8, SEC), jnp.float32),
            dma((LOADS,)), dma((4,)), dma((CHUNKS,)), dma((CHUNKS,)), dma((CHUNKS,)), dma((4,)),
            dma((len(PHASES),)), dma((len(PHASES),)),
        ],
        compiler_params=pltpu.CompilerParams(
            collective_id=0, has_side_effects=True, vmem_limit_bytes=44 * 1024 * 1024
        ),
        cost_estimate=pl.CostEstimate(flops=8 * SEC**3, bytes_accessed=20 << 20, transcendentals=0),
    )(site_ops, left_live, right_live, state, left_env, right_env)
    return pl.pallas_call(
        finish_kernel,
        grid=(8,),
        out_shape=(
            jax.ShapeDtypeStruct((1, SEC, SEC), jnp.float32),
            jax.ShapeDtypeStruct((2,), jnp.float32),
        ),
        in_specs=[
            pl.BlockSpec((3, 8, 128), lambda i: (0, 0, 0)),
            pl.BlockSpec((SEC // 8, SEC), lambda i: (i, 0)),
            pl.BlockSpec((SEC // 8, SEC), lambda i: (i, 0)),
        ],
        out_specs=(pl.BlockSpec((1, SEC // 8, SEC), lambda i: (0, i, 0)), smem),
        cost_estimate=pl.CostEstimate(flops=3 * SEC**2, bytes_accessed=12 << 20, transcendentals=0),
    )(sums, image, masked)


def solution(mesh):
    in_specs = (
        P(("left", "right"), None, None),
        P(None, ("left", "right"), None, None),
        P(None, ("left", "right"), None, None),
        P(),
        P(),
        P(),
    )
    out_specs = (P(("left", "right"), None, None), P())
    return jax.shard_map(
        per_device, mesh=mesh, in_specs=in_specs, out_specs=out_specs, check_vma=False
    )
```

```python
import jax
import jax.numpy as jnp
from jax import lax
from jax.experimental import pallas as pl
from jax.experimental.pallas import tpu as pltpu
from jax.sharding import PartitionSpec as P

MESH = pl.DeviceIdType.MESH
BLOCK = 256
PAIR = 4
SEC = 1024
DEVICES = 128
CHUNK = 32
CHUNKS = SEC // CHUNK
MERGED_UP = 13
LOAD = 128
LOADS = SEC // LOAD
TILE = 256
TILES = SEC // TILE
PHASES = ((1, 8), (8, 16))
ROUNDS = 3


def own_block():
    return lax.axis_index("left") * 16 + lax.axis_index("right")


def place(block):
    block = lax.rem(block + DEVICES, DEVICES)
    return (lax.div(block, 16), lax.rem(block, 16))


def along_z(block, step, core):
    z = lax.rem(lax.div(block, 2), 4)
    return lax.div(block, 8) * 8 + lax.rem(z + step + 4, 4) * 2 + core


def group_peer(block, stride, size, step):
    digit = lax.rem(lax.div(block, stride), size)
    return block + (lax.rem(digit + step, size) - digit) * stride


def axis_distance(step, size):
    return min(step % size, size - step % size)


def phase_steps(phase):
    inner = 2 if phase == 0 else 4
    size = PHASES[phase][1]
    outer = size // inner
    steps = [(a, b) for a in range(outer) for b in range(inner) if a or b]
    return sorted(steps, key=lambda s: -(axis_distance(s[0], outer) + axis_distance(s[1], inner)))


def phase_peer(block, phase, step):
    inner = 2 if phase == 0 else 4
    stride, size = PHASES[phase]
    block = group_peer(block, stride, inner, step[1])
    return group_peer(block, stride * inner, size // inner, step[0])


def goes_up(chunk):
    return lax.div((chunk + 1) * MERGED_UP, CHUNKS) > lax.div(chunk * MERGED_UP, CHUNKS)


def step_kernel(
    site_hbm, left_hbm, right_hbm, state, left_env, right_env,
    image, masked, sums,
    site_ops, left_live, right_live,
    own, first, second, source, left_zero, left_one, right_zero, right_one, part,
    slots, share, small_sem, load_sem, env_sem, first_sem, second_sem, source_sem, send_sem, sum_send, sum_recv, near_sem,
):
    k = own_block()
    core = lax.rem(k, 2)
    is_low = core == 0
    is_high = core == 1

    small = [
        pltpu.make_async_copy(site_hbm, site_ops, small_sem.at[0]),
        pltpu.make_async_copy(left_hbm, left_live, small_sem.at[1]),
        pltpu.make_async_copy(right_hbm, right_live, small_sem.at[2]),
    ]
    for copy in small:
        copy.start()
    loads = [
        pltpu.make_async_copy(
            state.at[0, pl.ds(i * LOAD, LOAD)], masked.at[pl.ds(i * LOAD, LOAD)], load_sem.at[i]
        )
        for i in range(LOADS)
    ]
    for load in loads:
        load.start()
    envs = [
        pltpu.make_async_copy(right_env.at[1, 0], right_one, env_sem.at[0]),
        pltpu.make_async_copy(left_env.at[1, 0], left_one, env_sem.at[1]),
        pltpu.make_async_copy(right_env.at[0, 0], right_zero, env_sem.at[2]),
        pltpu.make_async_copy(left_env.at[0, 0], left_zero, env_sem.at[3]),
    ]

    barrier = pltpu.get_barrier_semaphore()

    def greet(block):
        pl.semaphore_signal(barrier, inc=1, device_id=place(block), device_id_type=MESH)

    def relay_of(merger):
        z = lax.rem(lax.div(merger, 2), 4)
        crossed = along_z(lax.rem(merger + 3, DEVICES), 1, 0)
        return jnp.where(z == 2, crossed, along_z(merger, -1, 0))

    z = lax.rem(lax.div(k, 2), 4)
    relay = relay_of(k)
    crossing = lax.rem(along_z(k, -1, 0) + DEVICES - 3, DEVICES)
    merger = jnp.where(z == 1, crossing, along_z(k, 1, 1))
    onward = merger + 3
    near = [
        along_z(k, 1, core), along_z(k, -1, core), group_peer(k, 1, 2, 1),
        group_peer(k, 8, 4, 1), group_peer(k, 8, 4, 3), group_peer(k, 32, 4, 1), group_peer(k, 32, 4, 3),
    ]

    greet(k - 1)
    greet(k - 2)

    @pl.when(is_low)
    def _():
        greet(merger)
        greet(relay_of(lax.rem(k - 3 + DEVICES, DEVICES)))

    @pl.when(is_high)
    def _():
        greet(k + 1)

    for block in near:
        greet(block)
    for env in envs:
        env.start()

    for copy in small:
        copy.wait()

    def weight(target, distance):
        target = lax.rem(target + DEVICES, DEVICES)
        pair = lax.rem(target, PAIR)
        entry = site_ops[0, pair, lax.rem(pair - distance + PAIR, PAIR)]
        return jnp.where(target >= distance, entry, 0.0)

    up_two = weight(k + 2, 2)
    up_three = weight(k + 2, 3)
    merge_own = jnp.where(is_low, up_two, weight(k + 3, 3))
    merge_other = jnp.where(is_low, up_three, weight(k + 3, 2))
    own_pair = lax.rem(k, PAIR)
    diagonal = site_ops[1, own_pair, own_pair]
    sector = lax.div(k, PAIR)
    rows = left_live[sector] * BLOCK
    columns = right_live[sector + lax.div(own_pair + 1, 2)] * BLOCK
    column_live = lax.broadcasted_iota(jnp.int32, (1, SEC), 1) < columns

    def live(first_row, count):
        return (
            lax.broadcasted_iota(jnp.int32, (count, 1), 0) + first_row < rows
        ) & column_live

    def chunk_of(ref, chunk):
        return ref.at[pl.ds(pl.multiple_of(chunk * CHUNK, CHUNK), CHUNK)]

    def send(src, dst, send_at, recv, chunk, target):
        pltpu.make_async_remote_copy(
            src_ref=chunk_of(src, chunk),
            dst_ref=chunk_of(dst, chunk),
            send_sem=send_sem.at[send_at],
            recv_sem=recv.at[chunk],
            device_id=place(target),
            device_id_type=MESH,
        ).start()

    def arrived(ref, recv, chunk):
        pltpu.make_async_copy(chunk_of(ref, chunk), chunk_of(ref, chunk), recv.at[chunk]).wait()

    def fold(values):
        return jnp.sum(values.reshape(-1, 8, SEC // 128, 128), axis=(0, 2))

    share[...] = jnp.zeros_like(share)
    for i in range(LOADS):
        loads[i].wait()
        at = pl.ds(i * LOAD, LOAD)
        values = jnp.where(live(i * LOAD, LOAD), masked[at], 0.0)
        masked[at] = values
        own[at] = values.astype(jnp.bfloat16)
        share[0] += jnp.sum((values * values).reshape(LOAD // 8, 8, SEC), axis=0)
        if i == 0:
            pl.semaphore_wait(barrier, 4 - core + len(near))

        @pl.loop(i * (LOAD // CHUNK), (i + 1) * (LOAD // CHUNK))
        def _(chunk):
            @pl.when(is_low)
            def _():
                send(own, first, 0, first_sem, chunk, k + 1)

                @pl.when(jnp.logical_not(goes_up(chunk)))
                def _():
                    send(own, second, 1, second_sem, chunk, k - 1)

            @pl.when(is_high & goes_up(chunk))
            def _():
                send(own, second, 1, second_sem, chunk, k + 1)

    def tile_at(index):
        return pl.ds(pl.multiple_of(index * TILE, TILE), TILE)

    def part_one(index):
        at = tile_at(index)
        part[at] = jnp.dot(
            own[at], right_one[...], preferred_element_type=jnp.float32
        ).astype(jnp.bfloat16)

    def image_one(index):
        at = tile_at(index)
        image[at] = diagonal * jnp.dot(left_one[at], part[...], preferred_element_type=jnp.float32)

    def exchange(chunk):
        up = goes_up(chunk)

        @pl.when(is_high)
        def _():
            arrived(first, first_sem, chunk)
            at = pl.ds(pl.multiple_of(chunk * CHUNK, CHUNK), CHUNK)
            first[at] = (
                up_two * own[at].astype(jnp.float32) + up_three * first[at].astype(jnp.float32)
            ).astype(jnp.bfloat16)
            send(first, source, 2, source_sem, chunk, k + 2)

        @pl.when(up == is_low)
        def _():
            arrived(second, second_sem, chunk)
            at = pl.ds(pl.multiple_of(chunk * CHUNK, CHUNK), CHUNK)
            second[at] = (
                merge_own * own[at].astype(jnp.float32)
                + merge_other * second[at].astype(jnp.float32)
            ).astype(jnp.bfloat16)

            @pl.when(is_low)
            def _():
                send(second, source, 2, source_sem, chunk, k + 2)

            @pl.when(is_high)
            def _():
                send(second, first, 3, first_sem, chunk, relay)

        @pl.when(is_low & jnp.logical_not(up))
        def _():
            arrived(first, first_sem, chunk)
            send(first, source, 3, source_sem, chunk, onward)

    def tell(round_sem):
        for block in near:
            pl.semaphore_signal(
                near_sem.at[round_sem], inc=1, device_id=place(block), device_id_type=MESH
            )

    def told(round_sem):
        pl.semaphore_wait(near_sem.at[round_sem], len(near))

    tell(0)

    @pl.loop(0, TILES)
    def _(index):
        @pl.when(index == 0)
        def _():
            envs[0].wait()
            envs[1].wait()
            envs[2].wait()
            envs[3].wait()

        part_one(index)
        exchange(2 * index)
        exchange(2 * index + 1)

    told(0)
    tell(1)

    @pl.loop(0, TILES)
    def _(index):
        image_one(index)
        exchange(2 * index + 8)
        exchange(2 * index + 9)

    per_tile = TILE // CHUNK

    def consume(index, last):
        @pl.loop(index * per_tile, (index + 1) * per_tile)
        def _(chunk):
            arrived(source, source_sem, chunk)

        piece = pl.ds(index * TILE, TILE)
        part[piece] = jnp.dot(
            source[piece], right_zero[...], preferred_element_type=jnp.float32
        ).astype(jnp.bfloat16)

        @pl.loop(0, TILES)
        def _(row):
            at = tile_at(row)
            values = image[at] + jnp.dot(
                left_zero[at, piece], part[piece], preferred_element_type=jnp.float32
            )
            if last:
                values = jnp.where(live(row * TILE, TILE), values, 0.0)
                share[1] += jnp.sum((values * masked[at]).reshape(TILE // 8, 8, SEC), axis=0)
                share[2] += jnp.sum((values * values).reshape(TILE // 8, 8, SEC), axis=0)
            image[at] = values

    told(1)
    tell(2)
    consume(0, False)

    @pl.loop(16, 24)
    def _(chunk):
        exchange(chunk)

    consume(1, False)

    @pl.loop(24, 32)
    def _(chunk):
        exchange(chunk)

    told(2)
    consume(2, False)
    consume(3, True)

    for phase, (stride, size) in enumerate(PHASES):
        digit = lax.rem(lax.div(k, stride), size)
        if phase == 0:
            total = jnp.sum(share[...].reshape(3, 8, SEC // 128, 128), axis=2)
        else:
            total = jnp.sum(slots[phase - 1, 0 : PHASES[phase - 1][1]], axis=0)
        slots[phase, digit] = total
        for step in phase_steps(phase):
            pltpu.make_async_remote_copy(
                src_ref=slots.at[phase, digit],
                dst_ref=slots.at[phase, digit],
                send_sem=sum_send.at[phase],
                recv_sem=sum_recv.at[phase],
                device_id=place(phase_peer(k, phase, step)),
                device_id_type=MESH,
            ).start()
        others = slots.at[phase, pl.ds(0, size - 1)]
        pltpu.make_async_copy(others, others, sum_recv.at[phase]).wait()
    total = jnp.sum(slots[len(PHASES) - 1, 0 : PHASES[-1][1]], axis=0)
    total = jnp.sum(jnp.sum(total, axis=2, keepdims=True), axis=1, keepdims=True)
    entries = float(DEVICES * SEC * SEC)
    start = total[0] / entries
    overlap = total[1] / entries
    square = total[2] / entries
    scale = 1.0 / jnp.sqrt(start + 1e-06)
    slope = scale * scale * overlap
    rest = square - 2.0 * slope * overlap + slope * slope * start
    beta = jnp.sqrt(scale * scale * jnp.maximum(rest, 0.0) + 1e-06)
    sums[0] = jnp.broadcast_to(slope, (8, 128))
    sums[1] = jnp.broadcast_to(scale / beta, (8, 128))
    sums[2] = jnp.broadcast_to(beta, (8, 128))

    for phase, (stride, size) in enumerate(PHASES):
        others = slots.at[phase, pl.ds(0, size - 1)]
        pltpu.make_async_copy(others, others, sum_send.at[phase]).wait()

    def sent(flow, chunks):
        piece = own.at[pl.ds(0, chunks * CHUNK)]
        pltpu.make_async_copy(piece, piece, send_sem.at[flow]).wait()

    @pl.when(is_low)
    def _():
        sent(0, CHUNKS)
        sent(1, CHUNKS - MERGED_UP)
        sent(2, MERGED_UP)
        sent(3, CHUNKS - MERGED_UP)

    @pl.when(is_high)
    def _():
        sent(1, MERGED_UP)
        sent(2, CHUNKS)
        sent(3, CHUNKS - MERGED_UP)


def finish_kernel(sums, image, masked, next_vector, coefficients, result, sem):
    slope = sums[0, 0:1, 0:1]
    gain = sums[1, 0:1, 0:1]
    copies = []
    for i in range(LOADS):
        at = pl.ds(i * LOAD, LOAD)
        result[at] = (image[at] - slope * masked[at]) * gain
        copy = pltpu.make_async_copy(result.at[at], next_vector.at[0, at], sem.at[i])
        copy.start()
        copies.append(copy)
    coefficients[0] = jnp.max(sums[0])
    coefficients[1] = jnp.max(sums[2])
    for copy in copies:
        copy.wait()


def per_device(state, left_env, right_env, site_ops, left_live, right_live):
    hbm = pl.BlockSpec(memory_space=pltpu.HBM)
    smem = pl.BlockSpec(memory_space=pltpu.SMEM)
    vmem = pl.BlockSpec(memory_space=pltpu.VMEM)
    block = pltpu.VMEM((SEC, SEC), jnp.bfloat16)
    dma = pltpu.SemaphoreType.DMA
    state, left_env, right_env, site_ops, left_live, right_live = (
        pltpu.with_memory_space_constraint(array, pltpu.HBM)
        for array in (state, left_env, right_env, site_ops, left_live, right_live)
    )
    image, masked, sums = pl.pallas_call(
        step_kernel,
        out_shape=(
            jax.ShapeDtypeStruct((SEC, SEC), jnp.float32),
            jax.ShapeDtypeStruct((SEC, SEC), jnp.float32),
            jax.ShapeDtypeStruct((3, 8, 128), jnp.float32),
        ),
        in_specs=[hbm] * 6,
        out_specs=(vmem, vmem, vmem),
        scratch_shapes=[
            pltpu.SMEM(site_ops.shape, jnp.float32),
            pltpu.SMEM(left_live.shape, jnp.int32),
            pltpu.SMEM(right_live.shape, jnp.int32),
            block, block, block, block, block, block, block, block, block,
            pltpu.VMEM((len(PHASES), max(size for _, size in PHASES), 3, 8, 128), jnp.float32),
            pltpu.VMEM((3, 8, SEC), jnp.float32),
            dma((3,)), dma((LOADS,)), dma((4,)), dma((CHUNKS,)), dma((CHUNKS,)), dma((CHUNKS,)), dma((4,)),
            dma((len(PHASES),)), dma((len(PHASES),)),
            pltpu.SemaphoreType.REGULAR((ROUNDS,)),
        ],
        compiler_params=pltpu.CompilerParams(
            collective_id=0, has_side_effects=True, vmem_limit_bytes=44 * 1024 * 1024
        ),
        cost_estimate=pl.CostEstimate(flops=8 * SEC**3, bytes_accessed=20 << 20, transcendentals=0),
    )(site_ops, left_live, right_live, state, left_env, right_env)
    return pl.pallas_call(
        finish_kernel,
        out_shape=(
            jax.ShapeDtypeStruct((1, SEC, SEC), jnp.float32),
            jax.ShapeDtypeStruct((2,), jnp.float32),
        ),
        in_specs=[vmem, vmem, vmem],
        out_specs=(hbm, smem),
        scratch_shapes=[pltpu.VMEM((SEC, SEC), jnp.float32), dma((LOADS,))],
        compiler_params=pltpu.CompilerParams(vmem_limit_bytes=16 * 1024 * 1024),
        cost_estimate=pl.CostEstimate(flops=3 * SEC**2, bytes_accessed=4 << 20, transcendentals=0),
    )(sums, image, masked)


def solution(mesh):
    in_specs = (
        P(("left", "right"), None, None),
        P(None, ("left", "right"), None, None),
        P(None, ("left", "right"), None, None),
        P(),
        P(),
        P(),
    )
    out_specs = (P(("left", "right"), None, None), P())
    return jax.shard_map(
        per_device, mesh=mesh, in_specs=in_specs, out_specs=out_specs, check_vma=False
    )
```

```python
import jax
import jax.numpy as jnp
from jax import lax
from jax.experimental import pallas as pl
from jax.experimental.pallas import tpu as pltpu
from jax.sharding import PartitionSpec as P

MESH = pl.DeviceIdType.MESH
BLOCK = 256
PAIR = 4
SEC = 1024
DEVICES = 128
CHUNK = 32
CHUNKS = SEC // CHUNK
MERGED_UP = (13, 13, 15, 15)
LOAD = 128
LOADS = SEC // LOAD
OUT = 64
TILE = 256
TILES = SEC // TILE
PHASES = ((1, 8), (8, 16))
ROUNDS = 3


def own_block():
    return lax.axis_index("left") * 16 + lax.axis_index("right")


def place(block):
    block = lax.rem(block + DEVICES, DEVICES)
    return (lax.div(block, 16), lax.rem(block, 16))


def along_z(block, step, core):
    z = lax.rem(lax.div(block, 2), 4)
    return lax.div(block, 8) * 8 + lax.rem(z + step + 4, 4) * 2 + core


def group_peer(block, stride, size, step):
    digit = lax.rem(lax.div(block, stride), size)
    return block + (lax.rem(digit + step, size) - digit) * stride


def axis_distance(step, size):
    return min(step % size, size - step % size)


def phase_steps(phase):
    inner = 2 if phase == 0 else 4
    size = PHASES[phase][1]
    outer = size // inner
    steps = [(a, b) for a in range(outer) for b in range(inner) if a or b]
    return sorted(steps, key=lambda s: -(axis_distance(s[0], outer) + axis_distance(s[1], inner)))


def phase_peer(block, phase, step):
    inner = 2 if phase == 0 else 4
    stride, size = PHASES[phase]
    block = group_peer(block, stride, inner, step[1])
    return group_peer(block, stride * inner, size // inner, step[0])


def target_z(target):
    return lax.rem(lax.div(lax.rem(target, DEVICES), 2), 4)


def goes_up(chunk, target):
    z = target_z(target)
    count = jnp.int32(MERGED_UP[0])
    for i in range(1, 4):
        count = jnp.where(z == i, MERGED_UP[i], count)
    return lax.div((chunk + 1) * count, CHUNKS) > lax.div(chunk * count, CHUNKS)


def step_kernel(
    site_hbm, left_hbm, right_hbm, state, left_env, right_env,
    image, masked, sums,
    site_ops, left_live, right_live,
    own, first, second, source, left_zero, left_one, right_zero, right_one, part,
    slots, share, small_sem, load_sem, env_sem, first_sem, second_sem, source_sem, send_sem, sum_send, sum_recv, near_sem,
):
    k = own_block()
    core = lax.rem(k, 2)
    is_low = core == 0
    is_high = core == 1

    barrier = pltpu.get_barrier_semaphore()

    def greet(block):
        pl.semaphore_signal(barrier, inc=1, device_id=place(block), device_id_type=MESH)

    def relay_of(merger):
        z = lax.rem(lax.div(merger, 2), 4)
        crossed = along_z(lax.rem(merger + 3, DEVICES), 1, 0)
        return jnp.where(z == 2, crossed, along_z(merger, -1, 0))

    z = lax.rem(lax.div(k, 2), 4)
    relay = relay_of(k)
    crossing = lax.rem(along_z(k, -1, 0) + DEVICES - 3, DEVICES)
    merger = jnp.where(z == 1, crossing, along_z(k, 1, 1))
    onward = lax.rem(merger + 3, DEVICES)
    target = k + 2 + core
    near = [
        along_z(k, 1, core), along_z(k, -1, core), group_peer(k, 1, 2, 1),
        group_peer(k, 8, 4, 1), group_peer(k, 8, 4, 3), group_peer(k, 32, 4, 1), group_peer(k, 32, 4, 3),
    ]

    greet(k - 1)
    greet(k - 2)

    @pl.when(is_low)
    def _():
        greet(merger)
        greet(relay_of(lax.rem(k - 3 + DEVICES, DEVICES)))

    @pl.when(is_high)
    def _():
        greet(k + 1)

    for block in near:
        greet(block)

    small = [
        pltpu.make_async_copy(site_hbm, site_ops, small_sem.at[0]),
        pltpu.make_async_copy(left_hbm, left_live, small_sem.at[1]),
        pltpu.make_async_copy(right_hbm, right_live, small_sem.at[2]),
    ]
    for copy in small:
        copy.start()
    loads = [
        pltpu.make_async_copy(
            state.at[0, pl.ds(i * LOAD, LOAD)], masked.at[pl.ds(i * LOAD, LOAD)], load_sem.at[i]
        )
        for i in range(LOADS)
    ]
    for load in loads:
        load.start()
    envs = [
        pltpu.make_async_copy(right_env.at[1, 0], right_one, env_sem.at[0]),
        pltpu.make_async_copy(left_env.at[1, 0], left_one, env_sem.at[1]),
        pltpu.make_async_copy(right_env.at[0, 0], right_zero, env_sem.at[2]),
        pltpu.make_async_copy(left_env.at[0, 0], left_zero, env_sem.at[3]),
    ]

    for copy in small:
        copy.wait()

    def weight(target, distance):
        target = lax.rem(target + DEVICES, DEVICES)
        pair = lax.rem(target, PAIR)
        entry = site_ops[0, pair, lax.rem(pair - distance + PAIR, PAIR)]
        return jnp.where(target >= distance, entry, 0.0)

    up_two = weight(k + 2, 2)
    up_three = weight(k + 2, 3)
    merge_own = jnp.where(is_low, up_two, weight(k + 3, 3))
    merge_other = jnp.where(is_low, up_three, weight(k + 3, 2))
    own_pair = lax.rem(k, PAIR)
    diagonal = site_ops[1, own_pair, own_pair]
    sector = lax.div(k, PAIR)
    rows = left_live[sector] * BLOCK
    columns = right_live[sector + lax.div(own_pair + 1, 2)] * BLOCK
    column_live = lax.broadcasted_iota(jnp.int32, (1, SEC), 1) < columns

    def live(first_row, count):
        return (
            lax.broadcasted_iota(jnp.int32, (count, 1), 0) + first_row < rows
        ) & column_live

    def chunk_of(ref, chunk):
        return ref.at[pl.ds(pl.multiple_of(chunk * CHUNK, CHUNK), CHUNK)]

    def send(src, dst, send_at, recv, chunk, target):
        pltpu.make_async_remote_copy(
            src_ref=chunk_of(src, chunk),
            dst_ref=chunk_of(dst, chunk),
            send_sem=send_sem.at[send_at],
            recv_sem=recv.at[chunk],
            device_id=place(target),
            device_id_type=MESH,
        ).start()

    def arrived(ref, recv, chunk):
        pltpu.make_async_copy(chunk_of(ref, chunk), chunk_of(ref, chunk), recv.at[chunk]).wait()

    def fold(values):
        return jnp.sum(values.reshape(-1, 8, SEC // 128, 128), axis=(0, 2))

    share[...] = jnp.zeros_like(share)
    for i in range(LOADS):
        loads[i].wait()
        at = pl.ds(i * LOAD, LOAD)
        values = jnp.where(live(i * LOAD, LOAD), masked[at], 0.0)
        masked[at] = values
        own[at] = values.astype(jnp.bfloat16)
        if i == 1:
            for env in envs:
                env.start()
        if i == 0:
            pl.semaphore_wait(barrier, 4 - core + len(near))

        @pl.loop(i * (LOAD // CHUNK), (i + 1) * (LOAD // CHUNK))
        def _(chunk):
            @pl.when(is_low)
            def _():
                send(own, first, 0, first_sem, chunk, k + 1)

                @pl.when(jnp.logical_not(goes_up(chunk, target)))
                def _():
                    send(own, second, 1, second_sem, chunk, k - 1)

            @pl.when(is_high & goes_up(chunk, target))
            def _():
                send(own, second, 1, second_sem, chunk, k + 1)

    def tile_at(index):
        return pl.ds(pl.multiple_of(index * TILE, TILE), TILE)

    def part_one(index):
        at = tile_at(index)
        values = masked[at]
        share[0] += jnp.sum((values * values).reshape(TILE // 8, 8, SEC), axis=0)
        part[at] = jnp.dot(
            own[at], right_one[...], preferred_element_type=jnp.float32
        ).astype(jnp.bfloat16)

    def image_one(index):
        at = tile_at(index)
        image[at] = diagonal * jnp.dot(left_one[at], part[...], preferred_element_type=jnp.float32)

    def exchange(chunk):
        up = goes_up(chunk, target)

        @pl.when(is_high)
        def _():
            arrived(first, first_sem, chunk)
            at = pl.ds(pl.multiple_of(chunk * CHUNK, CHUNK), CHUNK)
            first[at] = (
                up_two * own[at].astype(jnp.float32) + up_three * first[at].astype(jnp.float32)
            ).astype(jnp.bfloat16)
            send(first, source, 2, source_sem, chunk, k + 2)

        @pl.when(up == is_low)
        def _():
            arrived(second, second_sem, chunk)
            at = pl.ds(pl.multiple_of(chunk * CHUNK, CHUNK), CHUNK)
            second[at] = (
                merge_own * own[at].astype(jnp.float32)
                + merge_other * second[at].astype(jnp.float32)
            ).astype(jnp.bfloat16)

            @pl.when(is_low)
            def _():
                send(second, source, 2, source_sem, chunk, k + 2)

            @pl.when(is_high)
            def _():
                send(second, first, 3, first_sem, chunk, relay)

        @pl.when(is_low & jnp.logical_not(goes_up(chunk, onward)))
        def _():
            arrived(first, first_sem, chunk)
            send(first, source, 3, source_sem, chunk, onward)

    def tell(round_sem):
        for block in near:
            pl.semaphore_signal(
                near_sem.at[round_sem], inc=1, device_id=place(block), device_id_type=MESH
            )

    def told(round_sem):
        pl.semaphore_wait(near_sem.at[round_sem], len(near))

    tell(0)
    envs[0].wait()

    @pl.loop(0, TILES)
    def _(index):
        part_one(index)

        @pl.loop(index * (CHUNKS // 16), (index + 1) * (CHUNKS // 16))
        def _(chunk):
            exchange(chunk)

    told(0)
    tell(1)
    envs[1].wait()

    @pl.loop(0, TILES)
    def _(index):
        image_one(index)

        @pl.loop((index + 4) * (CHUNKS // 16), (index + 5) * (CHUNKS // 16))
        def _(chunk):
            exchange(chunk)

    def consume(start, count, last):
        @pl.loop(start // CHUNK, (start + count) // CHUNK)
        def _(chunk):
            arrived(source, source_sem, chunk)

        piece = pl.ds(start, count)
        part[piece] = jnp.dot(
            source[piece], right_zero[...], preferred_element_type=jnp.float32
        ).astype(jnp.bfloat16)

        @pl.loop(0, TILES)
        def _(row):
            at = tile_at(row)
            values = image[at] + jnp.dot(
                left_zero[at, piece], part[piece], preferred_element_type=jnp.float32
            )
            if last:
                values = jnp.where(live(row * TILE, TILE), values, 0.0)
                share[1] += jnp.sum((values * masked[at]).reshape(TILE // 8, 8, SEC), axis=0)
                share[2] += jnp.sum((values * values).reshape(TILE // 8, 8, SEC), axis=0)
            image[at] = values

    told(1)
    tell(2)
    envs[2].wait()
    envs[3].wait()
    consume(0, 256, False)

    @pl.loop(CHUNKS // 2, 3 * CHUNKS // 4)
    def _(chunk):
        exchange(chunk)

    consume(256, 256, False)

    @pl.loop(3 * CHUNKS // 4, CHUNKS)
    def _(chunk):
        exchange(chunk)

    told(2)
    peers = [
        [place(phase_peer(k, phase, step)) for step in phase_steps(phase)]
        for phase in range(len(PHASES))
    ]
    consume(512, 256, False)
    consume(768, 128, False)
    consume(896, 128, True)

    for phase, (stride, size) in enumerate(PHASES):
        digit = lax.rem(lax.div(k, stride), size)
        if phase == 0:
            total = jnp.sum(share[...].reshape(3, 8, SEC // 128, 128), axis=2)
        else:
            total = jnp.sum(slots[phase - 1, 0 : PHASES[phase - 1][1]], axis=0)
        slots[phase, digit] = total
        for peer in peers[phase]:
            pltpu.make_async_remote_copy(
                src_ref=slots.at[phase, digit],
                dst_ref=slots.at[phase, digit],
                send_sem=sum_send.at[phase],
                recv_sem=sum_recv.at[phase],
                device_id=peer,
                device_id_type=MESH,
            ).start()
        others = slots.at[phase, pl.ds(0, size - 1)]
        pltpu.make_async_copy(others, others, sum_recv.at[phase]).wait()
    total = jnp.sum(slots[len(PHASES) - 1, 0 : PHASES[-1][1]], axis=0)
    total = jnp.sum(jnp.sum(total, axis=2, keepdims=True), axis=1, keepdims=True)
    entries = float(DEVICES * SEC * SEC)
    start = total[0] / entries
    overlap = total[1] / entries
    square = total[2] / entries
    scale = 1.0 / jnp.sqrt(start + 1e-06)
    slope = scale * scale * overlap
    rest = square - 2.0 * slope * overlap + slope * slope * start
    beta = jnp.sqrt(scale * scale * jnp.maximum(rest, 0.0) + 1e-06)
    sums[0] = jnp.broadcast_to(slope, (8, 128))
    sums[1] = jnp.broadcast_to(scale / beta, (8, 128))
    sums[2] = jnp.broadcast_to(beta, (8, 128))

    for phase, (stride, size) in enumerate(PHASES):
        others = slots.at[phase, pl.ds(0, size - 1)]
        pltpu.make_async_copy(others, others, sum_send.at[phase]).wait()

    def sent(flow, chunks):
        piece = own.at[pl.ds(0, chunks * CHUNK)]
        pltpu.make_async_copy(piece, piece, send_sem.at[flow]).wait()

    @pl.when(is_low)
    def _():
        sent(0, CHUNKS)

    @pl.when(is_high)
    def _():
        sent(2, CHUNKS)

    for i in range(4):
        up = MERGED_UP[i]

        @pl.when(is_low & (target_z(target) == i))
        def _():
            sent(1, CHUNKS - up)
            sent(2, up)

        @pl.when(is_low & (target_z(onward) == i))
        def _():
            sent(3, CHUNKS - up)

        @pl.when(is_high & (target_z(target) == i))
        def _():
            sent(1, up)
            sent(3, CHUNKS - up)


def finish_kernel(sums, image, masked, next_vector, coefficients, result, pair, sem, pair_sem):
    slope = sums[0, 0:1, 0:1]
    gain = sums[1, 0:1, 0:1]
    copies = []
    for i in range(SEC // OUT):
        at = pl.ds(i * OUT, OUT)
        result[at] = (image[at] - slope * masked[at]) * gain
        copy = pltpu.make_async_copy(result.at[at], next_vector.at[0, at], sem.at[i])
        copy.start()
        copies.append(copy)
        if i == 0:
            pair[0] = jnp.max(sums[0])
            pair[1] = jnp.max(sums[2])
            copy = pltpu.make_async_copy(pair, coefficients, pair_sem)
            copy.start()
            copies.append(copy)
    for copy in copies:
        copy.wait()


def per_device(state, left_env, right_env, site_ops, left_live, right_live):
    hbm = pl.BlockSpec(memory_space=pltpu.HBM)
    smem = pl.BlockSpec(memory_space=pltpu.SMEM)
    vmem = pl.BlockSpec(memory_space=pltpu.VMEM)
    block = pltpu.VMEM((SEC, SEC), jnp.bfloat16)
    dma = pltpu.SemaphoreType.DMA
    state, left_env, right_env, site_ops, left_live, right_live = (
        pltpu.with_memory_space_constraint(array, pltpu.HBM)
        for array in (state, left_env, right_env, site_ops, left_live, right_live)
    )
    image, masked, sums = pl.pallas_call(
        step_kernel,
        out_shape=(
            jax.ShapeDtypeStruct((SEC, SEC), jnp.float32),
            jax.ShapeDtypeStruct((SEC, SEC), jnp.float32),
            jax.ShapeDtypeStruct((3, 8, 128), jnp.float32),
        ),
        in_specs=[hbm] * 6,
        out_specs=(vmem, vmem, vmem),
        scratch_shapes=[
            pltpu.SMEM(site_ops.shape, jnp.float32),
            pltpu.SMEM(left_live.shape, jnp.int32),
            pltpu.SMEM(right_live.shape, jnp.int32),
            block, block, block, block, block, block, block, block, block,
            pltpu.VMEM((len(PHASES), max(size for _, size in PHASES), 3, 8, 128), jnp.float32),
            pltpu.VMEM((3, 8, SEC), jnp.float32),
            dma((3,)), dma((LOADS,)), dma((4,)), dma((CHUNKS,)), dma((CHUNKS,)), dma((CHUNKS,)), dma((4,)),
            dma((len(PHASES),)), dma((len(PHASES),)),
            pltpu.SemaphoreType.REGULAR((ROUNDS,)),
        ],
        compiler_params=pltpu.CompilerParams(
            collective_id=0, has_side_effects=True, vmem_limit_bytes=44 * 1024 * 1024
        ),
        cost_estimate=pl.CostEstimate(flops=8 * SEC**3, bytes_accessed=20 << 20, transcendentals=0),
    )(site_ops, left_live, right_live, state, left_env, right_env)
    return pl.pallas_call(
        finish_kernel,
        out_shape=(
            jax.ShapeDtypeStruct((1, SEC, SEC), jnp.float32),
            jax.ShapeDtypeStruct((2,), jnp.float32),
        ),
        in_specs=[vmem, vmem, vmem],
        out_specs=(hbm, hbm),
        scratch_shapes=[
            pltpu.VMEM((SEC, SEC), jnp.float32), pltpu.SMEM((2,), jnp.float32),
            dma((SEC // OUT,)), dma,
        ],
        compiler_params=pltpu.CompilerParams(vmem_limit_bytes=16 * 1024 * 1024),
        cost_estimate=pl.CostEstimate(flops=3 * SEC**2, bytes_accessed=4 << 20, transcendentals=0),
    )(sums, image, masked)


def solution(mesh):
    in_specs = (
        P(("left", "right"), None, None),
        P(None, ("left", "right"), None, None),
        P(None, ("left", "right"), None, None),
        P(),
        P(),
        P(),
    )
    out_specs = (P(("left", "right"), None, None), P())
    return jax.shard_map(
        per_device, mesh=mesh, in_specs=in_specs, out_specs=out_specs, check_vma=False
    )
```

```python
import jax
import jax.numpy as jnp
from jax import lax
from jax.experimental import pallas as pl
from jax.experimental.pallas import tpu as pltpu
from jax.sharding import PartitionSpec as P

MESH = pl.DeviceIdType.MESH
BLOCK = 256
PAIR = 4
SEC = 1024
DEVICES = 128
CHUNK = 32
CHUNKS = SEC // CHUNK
MERGED_UP = (15, 14, 15, 15)
LOAD = 128
LOADS = SEC // LOAD
OUT = 64
TILE = 256
TILES = SEC // TILE
LAG = 3
PHASES = ((1, 8), (8, 16))
ROUNDS = 3


def own_block():
    return lax.axis_index("left") * 16 + lax.axis_index("right")


def place(block):
    block = lax.rem(block + DEVICES, DEVICES)
    return (lax.div(block, 16), lax.rem(block, 16))


def along_z(block, step, core):
    z = lax.rem(lax.div(block, 2), 4)
    return lax.div(block, 8) * 8 + lax.rem(z + step + 4, 4) * 2 + core


def group_peer(block, stride, size, step):
    digit = lax.rem(lax.div(block, stride), size)
    return block + (lax.rem(digit + step, size) - digit) * stride


def axis_distance(step, size):
    return min(step % size, size - step % size)


def phase_steps(phase):
    inner = 2 if phase == 0 else 4
    size = PHASES[phase][1]
    outer = size // inner
    steps = [(a, b) for a in range(outer) for b in range(inner) if a or b]
    return sorted(steps, key=lambda s: -(axis_distance(s[0], outer) + axis_distance(s[1], inner)))


def phase_peer(block, phase, step):
    inner = 2 if phase == 0 else 4
    stride, size = PHASES[phase]
    block = group_peer(block, stride, inner, step[1])
    return group_peer(block, stride * inner, size // inner, step[0])


def target_z(target):
    return lax.rem(lax.div(lax.rem(target, DEVICES), 2), 4)


def goes_up(chunk, target):
    z = target_z(target)
    count = jnp.int32(MERGED_UP[0])
    for i in range(1, 4):
        count = jnp.where(z == i, MERGED_UP[i], count)
    return lax.div((chunk + 1) * count, CHUNKS) > lax.div(chunk * count, CHUNKS)


def step_kernel(
    site_hbm, left_hbm, right_hbm, state, left_env, right_env,
    image, masked, sums,
    site_ops, left_live, right_live,
    own, first, second, source, left_zero, left_one, right_zero, right_one, part,
    slots, share, small_sem, load_sem, env_sem, first_sem, second_sem, source_sem, send_sem, sum_send, sum_recv, near_sem,
):
    k = own_block()
    core = lax.rem(k, 2)
    is_low = core == 0
    is_high = core == 1

    barrier = pltpu.get_barrier_semaphore()

    def greet(block):
        pl.semaphore_signal(barrier, inc=1, device_id=place(block), device_id_type=MESH)

    def relay_of(merger):
        z = lax.rem(lax.div(merger, 2), 4)
        crossed = along_z(lax.rem(merger + 3, DEVICES), 1, 0)
        return jnp.where(z == 2, crossed, along_z(merger, -1, 0))

    z = lax.rem(lax.div(k, 2), 4)
    relay = relay_of(k)
    crossing = lax.rem(along_z(k, -1, 0) + DEVICES - 3, DEVICES)
    merger = jnp.where(z == 1, crossing, along_z(k, 1, 1))
    onward = lax.rem(merger + 3, DEVICES)
    target = k + 2 + core
    near = [
        along_z(k, 1, core), along_z(k, -1, core), group_peer(k, 1, 2, 1),
        group_peer(k, 8, 4, 1), group_peer(k, 8, 4, 3), group_peer(k, 32, 4, 1), group_peer(k, 32, 4, 3),
    ]

    greet(k - 1)
    greet(k - 2)

    @pl.when(is_low)
    def _():
        greet(merger)
        greet(relay_of(lax.rem(k - 3 + DEVICES, DEVICES)))

    @pl.when(is_high)
    def _():
        greet(k + 1)

    for block in near:
        greet(block)

    small = [
        pltpu.make_async_copy(site_hbm, site_ops, small_sem.at[0]),
        pltpu.make_async_copy(left_hbm, left_live, small_sem.at[1]),
        pltpu.make_async_copy(right_hbm, right_live, small_sem.at[2]),
    ]
    for copy in small:
        copy.start()
    loads = [
        pltpu.make_async_copy(
            state.at[0, pl.ds(i * LOAD, LOAD)], masked.at[pl.ds(i * LOAD, LOAD)], load_sem.at[i]
        )
        for i in range(LOADS)
    ]
    for load in loads:
        load.start()
    envs = [
        pltpu.make_async_copy(right_env.at[1, 0], right_one, env_sem.at[0]),
        pltpu.make_async_copy(left_env.at[1, 0], left_one, env_sem.at[1]),
        pltpu.make_async_copy(right_env.at[0, 0], right_zero, env_sem.at[2]),
        pltpu.make_async_copy(left_env.at[0, 0], left_zero, env_sem.at[3]),
    ]

    for copy in small:
        copy.wait()

    def weight(target, distance):
        target = lax.rem(target + DEVICES, DEVICES)
        pair = lax.rem(target, PAIR)
        entry = site_ops[0, pair, lax.rem(pair - distance + PAIR, PAIR)]
        return jnp.where(target >= distance, entry, 0.0)

    up_two = weight(k + 2, 2)
    up_three = weight(k + 2, 3)
    merge_own = jnp.where(is_low, up_two, weight(k + 3, 3))
    merge_other = jnp.where(is_low, up_three, weight(k + 3, 2))
    own_pair = lax.rem(k, PAIR)
    diagonal = site_ops[1, own_pair, own_pair]
    sector = lax.div(k, PAIR)
    rows = left_live[sector] * BLOCK
    columns = right_live[sector + lax.div(own_pair + 1, 2)] * BLOCK
    column_live = lax.broadcasted_iota(jnp.int32, (1, SEC), 1) < columns

    def live(first_row, count):
        return (
            lax.broadcasted_iota(jnp.int32, (count, 1), 0) + first_row < rows
        ) & column_live

    def chunk_of(ref, chunk):
        return ref.at[pl.ds(pl.multiple_of(chunk * CHUNK, CHUNK), CHUNK)]

    def send(src, dst, send_at, recv, chunk, target):
        pltpu.make_async_remote_copy(
            src_ref=chunk_of(src, chunk),
            dst_ref=chunk_of(dst, chunk),
            send_sem=send_sem.at[send_at],
            recv_sem=recv.at[chunk],
            device_id=place(target),
            device_id_type=MESH,
        ).start()

    def arrived(ref, recv, chunk):
        pltpu.make_async_copy(chunk_of(ref, chunk), chunk_of(ref, chunk), recv.at[chunk]).wait()

    def fold(values):
        return jnp.sum(values.reshape(-1, 8, SEC // 128, 128), axis=(0, 2))

    share[...] = jnp.zeros_like(share)
    for i in range(LOADS):
        loads[i].wait()
        at = pl.ds(i * LOAD, LOAD)
        values = jnp.where(live(i * LOAD, LOAD), masked[at], 0.0)
        masked[at] = values
        own[at] = values.astype(jnp.bfloat16)
        if i == 1:
            for env in envs:
                env.start()
        if i == 0:
            pl.semaphore_wait(barrier, 4 - core + len(near))

        @pl.loop(i * (LOAD // CHUNK), (i + 1) * (LOAD // CHUNK))
        def _(chunk):
            @pl.when(is_low)
            def _():
                send(own, first, 0, first_sem, chunk, k + 1)

                @pl.when(jnp.logical_not(goes_up(chunk, target)))
                def _():
                    send(own, second, 1, second_sem, chunk, k - 1)

            @pl.when(is_high & goes_up(chunk, target))
            def _():
                send(own, second, 1, second_sem, chunk, k + 1)

    def tile_at(index):
        return pl.ds(pl.multiple_of(index * TILE, TILE), TILE)

    def part_one(index):
        at = tile_at(index)
        values = masked[at]
        share[0] += jnp.sum((values * values).reshape(TILE // 8, 8, SEC), axis=0)
        part[at] = jnp.dot(
            own[at], right_one[...], preferred_element_type=jnp.float32
        ).astype(jnp.bfloat16)

    def image_one(index):
        at = tile_at(index)
        image[at] = diagonal * jnp.dot(left_one[at], part[...], preferred_element_type=jnp.float32)

    def pass_on(chunk):
        @pl.when(jnp.logical_not(goes_up(chunk, onward)))
        def _():
            arrived(first, first_sem, chunk)
            send(first, source, 3, source_sem, chunk, onward)

    def exchange(chunk):
        up = goes_up(chunk, target)

        @pl.when(is_high)
        def _():
            arrived(first, first_sem, chunk)
            at = pl.ds(pl.multiple_of(chunk * CHUNK, CHUNK), CHUNK)
            first[at] = (
                up_two * own[at].astype(jnp.float32) + up_three * first[at].astype(jnp.float32)
            ).astype(jnp.bfloat16)
            send(first, source, 2, source_sem, chunk, k + 2)

        @pl.when(up == is_low)
        def _():
            arrived(second, second_sem, chunk)
            at = pl.ds(pl.multiple_of(chunk * CHUNK, CHUNK), CHUNK)
            second[at] = (
                merge_own * own[at].astype(jnp.float32)
                + merge_other * second[at].astype(jnp.float32)
            ).astype(jnp.bfloat16)

            @pl.when(is_low)
            def _():
                send(second, source, 2, source_sem, chunk, k + 2)

            @pl.when(is_high)
            def _():
                send(second, first, 3, first_sem, chunk, relay)

        @pl.when((chunk >= LAG) & is_low)
        def _():
            pass_on(jnp.maximum(chunk - LAG, 0))

    def tell(round_sem):
        for block in near:
            pl.semaphore_signal(
                near_sem.at[round_sem], inc=1, device_id=place(block), device_id_type=MESH
            )

    def told(round_sem):
        pl.semaphore_wait(near_sem.at[round_sem], len(near))

    tell(0)
    envs[0].wait()

    @pl.loop(0, TILES)
    def _(index):
        part_one(index)

        @pl.loop(index * (CHUNKS // 16), (index + 1) * (CHUNKS // 16))
        def _(chunk):
            exchange(chunk)

    told(0)
    tell(1)
    envs[1].wait()

    @pl.loop(0, TILES)
    def _(index):
        image_one(index)

        @pl.loop((index + 4) * (CHUNKS // 16), (index + 5) * (CHUNKS // 16))
        def _(chunk):
            exchange(chunk)

    def consume(start, count, last):
        @pl.loop(start // CHUNK, (start + count) // CHUNK)
        def _(chunk):
            arrived(source, source_sem, chunk)

        piece = pl.ds(start, count)
        part[piece] = jnp.dot(
            source[piece], right_zero[...], preferred_element_type=jnp.float32
        ).astype(jnp.bfloat16)

        @pl.loop(0, TILES)
        def _(row):
            at = tile_at(row)
            values = image[at] + jnp.dot(
                left_zero[at, piece], part[piece], preferred_element_type=jnp.float32
            )
            if last:
                values = jnp.where(live(row * TILE, TILE), values, 0.0)
                share[1] += jnp.sum((values * masked[at]).reshape(TILE // 8, 8, SEC), axis=0)
                share[2] += jnp.sum((values * values).reshape(TILE // 8, 8, SEC), axis=0)
            image[at] = values

    told(1)
    tell(2)
    envs[2].wait()
    envs[3].wait()
    @pl.loop(16, 20)
    def _(chunk):
        exchange(chunk)

    consume(0, 256, False)

    @pl.loop(20, 28)
    def _(chunk):
        exchange(chunk)

    consume(256, 256, False)

    @pl.loop(28, 32)
    def _(chunk):
        exchange(chunk)

    @pl.when(is_low)
    def _():
        @pl.loop(CHUNKS - LAG, CHUNKS)
        def _(chunk):
            pass_on(chunk)

    told(2)
    peers = [
        [place(phase_peer(k, phase, step)) for step in phase_steps(phase)]
        for phase in range(len(PHASES))
    ]
    consume(512, 256, False)
    consume(768, 128, False)
    consume(896, 128, True)

    for phase, (stride, size) in enumerate(PHASES):
        digit = lax.rem(lax.div(k, stride), size)
        if phase == 0:
            total = jnp.sum(share[...].reshape(3, 8, SEC // 128, 128), axis=2)
        else:
            total = jnp.sum(slots[phase - 1, 0 : PHASES[phase - 1][1]], axis=0)
        slots[phase, digit] = total
        for peer in peers[phase]:
            pltpu.make_async_remote_copy(
                src_ref=slots.at[phase, digit],
                dst_ref=slots.at[phase, digit],
                send_sem=sum_send.at[phase],
                recv_sem=sum_recv.at[phase],
                device_id=peer,
                device_id_type=MESH,
            ).start()
        others = slots.at[phase, pl.ds(0, size - 1)]
        pltpu.make_async_copy(others, others, sum_recv.at[phase]).wait()
    total = jnp.sum(slots[len(PHASES) - 1, 0 : PHASES[-1][1]], axis=0)
    total = jnp.sum(jnp.sum(total, axis=2, keepdims=True), axis=1, keepdims=True)
    entries = float(DEVICES * SEC * SEC)
    start = total[0] / entries
    overlap = total[1] / entries
    square = total[2] / entries
    scale = 1.0 / jnp.sqrt(start + 1e-06)
    slope = scale * scale * overlap
    rest = square - 2.0 * slope * overlap + slope * slope * start
    beta = jnp.sqrt(scale * scale * jnp.maximum(rest, 0.0) + 1e-06)
    sums[0] = jnp.broadcast_to(slope, (8, 128))
    sums[1] = jnp.broadcast_to(scale / beta, (8, 128))
    sums[2] = jnp.broadcast_to(beta, (8, 128))

    for phase, (stride, size) in enumerate(PHASES):
        others = slots.at[phase, pl.ds(0, size - 1)]
        pltpu.make_async_copy(others, others, sum_send.at[phase]).wait()

    def sent(flow, chunks):
        piece = own.at[pl.ds(0, chunks * CHUNK)]
        pltpu.make_async_copy(piece, piece, send_sem.at[flow]).wait()

    @pl.when(is_low)
    def _():
        sent(0, CHUNKS)

    @pl.when(is_high)
    def _():
        sent(2, CHUNKS)

    for i in range(4):
        up = MERGED_UP[i]

        @pl.when(is_low & (target_z(target) == i))
        def _():
            sent(1, CHUNKS - up)
            sent(2, up)

        @pl.when(is_low & (target_z(onward) == i))
        def _():
            sent(3, CHUNKS - up)

        @pl.when(is_high & (target_z(target) == i))
        def _():
            sent(1, up)
            sent(3, CHUNKS - up)


def finish_kernel(sums, image, masked, next_vector, coefficients, result, pair, sem, pair_sem):
    slope = sums[0, 0:1, 0:1]
    gain = sums[1, 0:1, 0:1]
    copies = []
    for i in range(SEC // OUT):
        at = pl.ds(i * OUT, OUT)
        result[at] = (image[at] - slope * masked[at]) * gain
        copy = pltpu.make_async_copy(result.at[at], next_vector.at[0, at], sem.at[i])
        copy.start()
        copies.append(copy)
        if i == 0:
            pair[0] = jnp.max(sums[0])
            pair[1] = jnp.max(sums[2])
            copy = pltpu.make_async_copy(pair, coefficients, pair_sem)
            copy.start()
            copies.append(copy)
    for copy in copies:
        copy.wait()


def per_device(state, left_env, right_env, site_ops, left_live, right_live):
    hbm = pl.BlockSpec(memory_space=pltpu.HBM)
    smem = pl.BlockSpec(memory_space=pltpu.SMEM)
    vmem = pl.BlockSpec(memory_space=pltpu.VMEM)
    block = pltpu.VMEM((SEC, SEC), jnp.bfloat16)
    dma = pltpu.SemaphoreType.DMA
    state, left_env, right_env, site_ops, left_live, right_live = (
        pltpu.with_memory_space_constraint(array, pltpu.HBM)
        for array in (state, left_env, right_env, site_ops, left_live, right_live)
    )
    image, masked, sums = pl.pallas_call(
        step_kernel,
        out_shape=(
            jax.ShapeDtypeStruct((SEC, SEC), jnp.float32),
            jax.ShapeDtypeStruct((SEC, SEC), jnp.float32),
            jax.ShapeDtypeStruct((3, 8, 128), jnp.float32),
        ),
        in_specs=[hbm] * 6,
        out_specs=(vmem, vmem, vmem),
        scratch_shapes=[
            pltpu.SMEM(site_ops.shape, jnp.float32),
            pltpu.SMEM(left_live.shape, jnp.int32),
            pltpu.SMEM(right_live.shape, jnp.int32),
            block, block, block, block, block, block, block, block, block,
            pltpu.VMEM((len(PHASES), max(size for _, size in PHASES), 3, 8, 128), jnp.float32),
            pltpu.VMEM((3, 8, SEC), jnp.float32),
            dma((3,)), dma((LOADS,)), dma((4,)), dma((CHUNKS,)), dma((CHUNKS,)), dma((CHUNKS,)), dma((4,)),
            dma((len(PHASES),)), dma((len(PHASES),)),
            pltpu.SemaphoreType.REGULAR((ROUNDS,)),
        ],
        compiler_params=pltpu.CompilerParams(
            collective_id=0, has_side_effects=True, vmem_limit_bytes=44 * 1024 * 1024
        ),
        cost_estimate=pl.CostEstimate(flops=8 * SEC**3, bytes_accessed=20 << 20, transcendentals=0),
    )(site_ops, left_live, right_live, state, left_env, right_env)
    return pl.pallas_call(
        finish_kernel,
        out_shape=(
            jax.ShapeDtypeStruct((1, SEC, SEC), jnp.float32),
            jax.ShapeDtypeStruct((2,), jnp.float32),
        ),
        in_specs=[vmem, vmem, vmem],
        out_specs=(hbm, hbm),
        scratch_shapes=[
            pltpu.VMEM((SEC, SEC), jnp.float32), pltpu.SMEM((2,), jnp.float32),
            dma((SEC // OUT,)), dma,
        ],
        compiler_params=pltpu.CompilerParams(vmem_limit_bytes=16 * 1024 * 1024),
        cost_estimate=pl.CostEstimate(flops=3 * SEC**2, bytes_accessed=4 << 20, transcendentals=0),
    )(sums, image, masked)


def solution(mesh):
    in_specs = (
        P(("left", "right"), None, None),
        P(None, ("left", "right"), None, None),
        P(None, ("left", "right"), None, None),
        P(),
        P(),
        P(),
    )
    out_specs = (P(("left", "right"), None, None), P())
    return jax.shard_map(
        per_device, mesh=mesh, in_specs=in_specs, out_specs=out_specs, check_vma=False
    )
```
